256 devices in a mesh: scen: 4 (over z_lo, core), tile: 64 (over z_hi, x, y).
Axes of the slice: x: 4, y: 4, z: 8 (z_hi: 4, z_lo: 2; z = z_hi * 2 + z_lo), core: 2. Of those that a mesh axis runs over, the one named last changes fastest.
Arguments:
- initial_heads: bfloat16 [512, 256, 512], P('scen', 'tile'), may hold values from -6 to 6
- diffusivity: float32 [256, 512], P('tile'), may hold values from 0.03 to 0.24
- recharge_map: float32 [256, 512], P('tile'), may hold values from 0.2 to 2
- rate_table: float32 [8, 4], replicated, may hold values from 0 to 0.5
- recharge_ids: int32 [512], P('scen'), may hold values from 0 to 7
- monitor_cells: int32 [4096], P('tile'), may hold values from 0 to 2047, as said below
- well_cells: int32 [512], P('tile'), may hold values from 0 to 2047, as said below
- targets: float32 [4096], P('tile'), may hold values from -3 to 3
- w_in: bfloat16 [4096, 2048], P('tile'), may hold values from -0.09375 to 0.09375
- b_in: float32 [2048], P('tile'), may hold values from -3 to 3
- w_mid: bfloat16 [2048, 2048], P('tile'), may hold values from -0.125 to 0.125
- b_mid: float32 [2048], P('tile'), may hold values from -3 to 3
- w_out: bfloat16 [2048, 512], P('tile'), may hold values from -0.125 to 0.125
- b_out: float32 [512], P('tile'), may hold values from -3 to 3
Outputs:
- final_heads: bfloat16 [512, 4096], P('scen', 'tile')
- g_w_in: float32 [4096, 2048], P('tile')
- g_b_in: float32 [2048], P('tile')
- g_w_mid: float32 [2048, 2048], P('tile')
- g_b_mid: float32 [2048], P('tile')
- g_w_out: float32 [2048, 512], P('tile')
- g_b_out: float32 [512], P('tile')
The draws below stay inside these ranges and needn't reach their ends.
Inputs may be any that keep to these rules, and one draw needn't show every extreme that they name: `monitor_cells`: each entry is a cell of its own slab, numbered row by row over its 4 x 512 cells. `well_cells`: each entry is a cell of its own slab, numbered row by row over its 4 x 512 cells.
All inputs are finite; a program needn't handle non-finite values.
Results may differ from the reference program's by a relative error of at most 0.009.
Values may be sent and summed in bfloat16 or wider, within the bound.
No kernel may reach another device: no remote copies, remote signals or barrier semaphores. Data moves between devices by JAX's collectives and lax.ppermute only.
A program may use at most 64 MiB of HBM per device.

```python
import math
import jax
import jax.numpy as jnp
from jax import lax

MONITORS = 4096
HIDDEN_SIZE = 2048
WELLS = 512
CR = 4
CW = 512
STEPS = 4
NREC = 8
ALL_MEMBERS = 512
GRID_ROWS = 256
N_TILE = 64


def shared_columns(key):
    return jax.random.randint(key, (N_TILE, 2), 0, CW, dtype=jnp.int32)


def draw_well_cells(key, part):
    columns = shared_columns(key)
    key = jax.random.fold_in(key, 11)
    per_slab = WELLS // N_TILE
    random_cells = jax.random.randint(key, (N_TILE, per_slab), 0, CR * CW, dtype=jnp.int32)
    slot = jnp.arange(per_slab, dtype=jnp.int32)[None, :]
    first_row = columns[:, 0][:, None]
    last_row = ((CR - 1) * CW + columns[:, 1])[:, None]
    cells = jnp.where(slot == 0, first_row, jnp.where(slot == 1, last_row, random_cells))
    return cells.reshape(WELLS).astype(jnp.int32)


def draw_monitor_cells(key, part):
    columns = shared_columns(key)
    key = jax.random.fold_in(key, 12)
    per_slab = MONITORS // N_TILE
    random_cells = jax.random.randint(key, (N_TILE, per_slab), 0, CR * CW, dtype=jnp.int32)
    slot = jnp.arange(per_slab, dtype=jnp.int32)[None, :]
    next_cols = jnp.roll(columns[:, 0], -1)
    prev_cols = jnp.roll(columns[:, 1], 1)
    last_row = ((CR - 1) * CW + next_cols)[:, None]
    first_row = prev_cols[:, None]
    cells = jnp.where(slot == 0, last_row, jnp.where(slot == 1, first_row, random_cells))
    return cells.reshape(MONITORS).astype(jnp.int32)


def place_ends(drawn, own_key, least, largest):
    shape = drawn.shape
    place = [jax.random.randint(jax.random.fold_in(own_key, axis), (), 0, shape[axis]) for axis in range(len(shape))]
    drawn = drawn.at[tuple(place)].set(least)
    longest = shape.index(max(shape))
    place[longest] = (place[longest] + 1) % shape[longest]
    return drawn.at[tuple(place)].set(largest)


def levels(stream_key, shape, split, smallest, largest):
    def one(axis_at, blocks):
        heights = jax.random.uniform(jax.random.fold_in(jax.random.fold_in(stream_key, 6), axis_at), (blocks,), jnp.float32, smallest / len(split), largest / len(split))
        return jnp.repeat(jnp.exp(heights), shape[axis_at] // blocks).reshape((-1,) + (1,) * (len(shape) - axis_at - 1))

    gain = one(*split[0])
    for cut in split[1:]:
        gain = gain * one(*cut)
    return gain


def centred(own_key, extent, deviation, most, cuts=(), held_as=jnp.bfloat16):
    values = jax.random.normal(own_key, extent, jnp.float32) * deviation
    if len(cuts) > 0:
        values = levels(own_key, extent, cuts, -0.22, 0.18) * values
    return jnp.clip(values, min=-most, max=most).astype(held_as)


def setup_inputs(seed: int = 0) -> dict:
    arg_keys = jax.random.split(jax.random.key(seed), 15)
    initial_heads = centred(arg_keys[0], (ALL_MEMBERS, GRID_ROWS, CW), 1.0, 6.0, ((0, 4), (1, 64)))
    diffusivity = jnp.clip(0.03 + 0.21 * jax.random.uniform(arg_keys[1], (GRID_ROWS, CW), jnp.float32) ** levels(arg_keys[1], (GRID_ROWS, CW), ((0, 64),), -0.2, 0.2), 0.03, 0.24)
    recharge_map = jnp.clip(jnp.exp(math.log(2.0) - 2.3025851 * jax.random.uniform(arg_keys[2], (GRID_ROWS, CW), jnp.float32) ** levels(arg_keys[2], (GRID_ROWS, CW), ((0, 64),), -0.2, 0.2)), 0.2, 2.0)
    rate_table = jnp.clip(jax.random.uniform(arg_keys[3], (NREC, STEPS), jnp.float32, 0.0, 0.5), 0.0, 0.5)
    recharge_ids = place_ends(jax.random.randint(arg_keys[4], (ALL_MEMBERS,), 0, NREC), jax.random.fold_in(arg_keys[4], 1), 0, NREC - 1).astype(jnp.int32)
    monitor_cells = draw_monitor_cells(jax.random.fold_in(arg_keys[14], 71), 0)
    well_cells = draw_well_cells(jax.random.fold_in(arg_keys[14], 71), 0)
    targets = centred(arg_keys[7], (MONITORS,), 0.5, 3.0, ((0, 64),), jnp.float32)
    w_in = centred(arg_keys[8], (MONITORS, HIDDEN_SIZE), MONITORS ** -0.5, 0.09375, ((0, 64),))
    b_in = centred(arg_keys[9], (HIDDEN_SIZE,), 0.5, 3.0, ((0, 64),), jnp.float32)
    w_mid = centred(arg_keys[10], (HIDDEN_SIZE, HIDDEN_SIZE), HIDDEN_SIZE ** -0.5, 0.125, ((0, 64),))
    b_mid = centred(arg_keys[11], (HIDDEN_SIZE,), 0.5, 3.0, ((0, 64),), jnp.float32)
    w_out = centred(arg_keys[12], (HIDDEN_SIZE, WELLS), HIDDEN_SIZE ** -0.5, 0.125, ((0, 64),))
    b_out = centred(arg_keys[13], (WELLS,), 0.5, 3.0, ((0, 64),), jnp.float32)
    return {"initial_heads": initial_heads, "diffusivity": diffusivity, "recharge_map": recharge_map, "rate_table": rate_table, "recharge_ids": recharge_ids, "monitor_cells": monitor_cells, "well_cells": well_cells, "targets": targets, "w_in": w_in, "b_in": b_in, "w_mid": w_mid, "b_mid": b_mid, "w_out": w_out, "b_out": b_out}


def laplace(field):
    padded = jnp.pad(field, ((0, 0), (1, 1), (1, 1)))
    return padded[:, 2:, 1:-1] + padded[:, :-2, 1:-1] + padded[:, 1:-1, 2:] + padded[:, 1:-1, :-2] - 4.0 * field

def widedot(left, right):
    return jnp.dot(left.astype(jnp.float32), right.astype(jnp.float32), precision=lax.Precision.HIGHEST)

def reference(initial_heads, diffusivity, recharge_map, rate_table, recharge_ids, monitor_cells, well_cells, targets, w_in, b_in, w_mid, b_mid, w_out, b_out):
    members = initial_heads.shape[0]
    cells = CR * CW
    mon_global = (jnp.arange(MONITORS, dtype=jnp.int32) // (MONITORS // N_TILE) * cells + monitor_cells).astype(jnp.int32)
    well_global = (jnp.arange(WELLS, dtype=jnp.int32) // (WELLS // N_TILE) * cells + well_cells).astype(jnp.int32)
    total_cells = N_TILE * cells
    observed = initial_heads.reshape(members, total_cells)[:, mon_global]
    act1 = jnp.tanh(widedot(observed, w_in) + b_in).astype(jnp.bfloat16)
    act2 = jnp.tanh(widedot(act1, w_mid) + b_mid).astype(jnp.bfloat16)
    pre3 = widedot(act2, w_out) + b_out
    rates = 0.5 * jax.nn.softplus(pre3)
    sink = jnp.zeros((members, total_cells), jnp.float32).at[:, well_global].add(rates).reshape(initial_heads.shape)
    monthly = rate_table[recharge_ids]
    heads = initial_heads
    for step in range(STEPS):
        current = heads.astype(jnp.float32)
        heads = (current + diffusivity * laplace(current) + monthly[:, step][:, None, None] * recharge_map - sink).astype(jnp.bfloat16)
    final_heads = heads.reshape(members, total_cells)[:, mon_global]
    spread = (final_heads.astype(jnp.float32) - targets) / math.sqrt(members)
    adjoint = jnp.zeros((members, total_cells), jnp.float32).at[:, mon_global].add(spread).reshape(initial_heads.shape)
    total = adjoint
    for step in range(STEPS - 1):
        adjoint = adjoint + laplace(diffusivity * adjoint)
        total = total + adjoint
    well_grad = -total.reshape(members, total_cells)[:, well_global]
    g3 = (well_grad * 0.5 * jax.nn.sigmoid(pre3)).astype(jnp.bfloat16)
    g_w_out = widedot(act2.T, g3)
    g_b_out = lax.optimization_barrier(jnp.sum(g3.astype(jnp.float32), axis=0))
    act2_f = act2.astype(jnp.float32)
    g2 = (widedot(g3, w_out.T) * (1.0 - act2_f * act2_f)).astype(jnp.bfloat16)
    g_w_mid = widedot(act1.T, g2)
    g_b_mid = lax.optimization_barrier(jnp.sum(g2.astype(jnp.float32), axis=0))
    act1_f = act1.astype(jnp.float32)
    g1 = (widedot(g2, w_mid.T) * (1.0 - act1_f * act1_f)).astype(jnp.bfloat16)
    g_w_in = widedot(observed.T, g1)
    g_b_in = lax.optimization_barrier(jnp.sum(g1.astype(jnp.float32), axis=0))
    return (final_heads, g_w_in, g_b_in, g_w_mid, g_b_mid, g_w_out, g_b_out)
```

```python
import math

import jax
import jax.numpy as jnp
from jax import lax
from jax.sharding import PartitionSpec as P


def with_halo(block, sides, width):
    for axis, dim in sides:
        count = lax.axis_size(axis)
        forward = [(i, i + 1) for i in range(count - 1)]
        backward = [(target, source) for source, target in forward]
        low = lax.ppermute(
            lax.slice_in_dim(block, block.shape[dim] - width, None, axis=dim), axis, forward
        )
        high = lax.ppermute(lax.slice_in_dim(block, 0, width, axis=dim), axis, backward)
        block = jnp.concatenate([low, block, high], axis=dim)
    return block


def laplace(padded_rows, center):
    padded = jnp.pad(padded_rows, ((0, 0), (0, 0), (1, 1)))
    return (
        padded[:, 2:, 1:-1]
        + padded[:, :-2, 1:-1]
        + padded[:, 1:-1, 2:]
        + padded[:, 1:-1, :-2]
        - 4.0 * center
    )


def scatter_sum(terms):
    count = lax.axis_size("tile")
    parts = terms.reshape((count, terms.shape[0] // count) + terms.shape[1:])
    parts = lax.all_to_all(parts, "tile", 0, 0, tiled=True)
    return jnp.sum(parts, axis=0)


def gather(block):
    count = lax.axis_size("tile")
    copies = jnp.broadcast_to(block[None], (count,) + block.shape)
    got = lax.all_to_all(copies, "tile", 0, 0, tiled=True)
    return got.reshape((count * block.shape[0],) + block.shape[1:])


def column_term(weight, activ):
    return lax.dot_general(
        weight, activ, (((0,), (0,)), ((), ())), preferred_element_type=jnp.float32
    )


def back_step(weight, activ, piece):
    g_act = jnp.dot(weight, piece, preferred_element_type=jnp.float32)
    block = lax.dot_general(
        activ, piece, (((1,), (1,)), ((), ())), preferred_element_type=jnp.float32
    )
    return (g_act, block)


def per_device(
    initial_heads,
    diffusivity,
    recharge_map,
    rate_table,
    recharge_ids,
    monitor_cells,
    well_cells,
    targets,
    w_in,
    b_in,
    w_mid,
    b_mid,
    w_out,
    b_out,
):
    members, rows, cols = initial_heads.shape
    cells = rows * cols
    grand = members * lax.axis_size("scen")
    steps = rate_table.shape[1]
    positions = jnp.arange(cells, dtype=jnp.int32)
    monitor_hot = (monitor_cells[:, None] == positions[None, :]).astype(jnp.float32)
    monitor_pick = monitor_hot.astype(jnp.bfloat16)
    well_hot = (well_cells[:, None] == positions[None, :]).astype(jnp.float32)
    observed = lax.dot_general(
        initial_heads.reshape(members, cells),
        monitor_pick,
        (((1,), (1,)), ((), ())),
        preferred_element_type=jnp.float32,
    ).astype(jnp.bfloat16)
    first_pre = scatter_sum(
        lax.dot_general(
            w_in, observed, (((0,), (1,)), ((), ())), preferred_element_type=jnp.float32
        )
    )
    act1 = jnp.tanh(first_pre + b_in[:, None]).astype(jnp.bfloat16)
    middle_pre = scatter_sum(column_term(w_mid, act1))
    act2 = jnp.tanh(middle_pre + b_mid[:, None]).astype(jnp.bfloat16)
    pre3 = (
        scatter_sum(column_term(w_out, act2))
        + b_out[:, None]
    )
    rates = 0.5 * jax.nn.softplus(pre3)
    sink = lax.dot_general(
        rates, well_hot, (((0,), (0,)), ((), ())), precision=lax.Precision.HIGHEST
    ).reshape(members, rows, cols)
    codes = jnp.arange(rate_table.shape[0], dtype=jnp.int32)
    pattern_hot = (recharge_ids[:, None] == codes[None, :]).astype(jnp.float32)
    monthly = jnp.dot(pattern_hot, rate_table, precision=lax.Precision.HIGHEST)
    heads = initial_heads
    for step in range(steps):
        padded = with_halo(heads, (("tile", 1),), 1)
        current = heads.astype(jnp.float32)
        heads = (
            current
            + diffusivity * laplace(padded.astype(jnp.float32), current)
            + monthly[:, step][:, None, None] * recharge_map
            - sink
        ).astype(jnp.bfloat16)
    final_heads = lax.dot_general(
        heads.reshape(members, cells),
        monitor_pick,
        (((1,), (1,)), ((), ())),
        preferred_element_type=jnp.float32,
    ).astype(jnp.bfloat16)
    spread = (final_heads.astype(jnp.float32) - targets[None, :]) / math.sqrt(grand)
    adjoint = jnp.dot(spread, monitor_hot, precision=lax.Precision.HIGHEST).reshape(
        members, rows, cols
    )
    total = adjoint
    for step in range(steps - 1):
        weighted = diffusivity * adjoint
        padded = with_halo(weighted, (("tile", 1),), 1)
        adjoint = adjoint + laplace(padded, weighted)
        total = total + adjoint
    well_grad = -lax.dot_general(
        well_hot,
        total.reshape(members, cells),
        (((1,), (1,)), ((), ())),
        precision=lax.Precision.HIGHEST,
    )
    g3 = (well_grad * 0.5 * jax.nn.sigmoid(pre3)).astype(jnp.bfloat16)
    g_b_out = jnp.sum(g3.astype(jnp.float32), axis=1)
    g_act2, g_w_out = back_step(w_out, act2, gather(g3))
    act2_f = act2.astype(jnp.float32)
    g2 = (g_act2 * (1.0 - act2_f * act2_f)).astype(jnp.bfloat16)
    g_b_mid = jnp.sum(g2.astype(jnp.float32), axis=1)
    g_act1, g_w_mid = back_step(w_mid, act1, gather(g2))
    act1_f = act1.astype(jnp.float32)
    g1 = (g_act1 * (1.0 - act1_f * act1_f)).astype(jnp.bfloat16)
    g_b_in = jnp.sum(g1.astype(jnp.float32), axis=1)
    g_w_in = lax.dot_general(
        observed,
        gather(g1),
        (((0,), (1,)), ((), ())),
        preferred_element_type=jnp.float32,
    )
    g_w_in, g_b_in, g_w_mid, g_b_mid, g_w_out, g_b_out = lax.psum(
        (g_w_in, g_b_in, g_w_mid, g_b_mid, g_w_out, g_b_out), "scen"
    )
    return (final_heads, g_w_in, g_b_in, g_w_mid, g_b_mid, g_w_out, g_b_out)


def solution(mesh):
    return jax.shard_map(
        per_device,
        mesh=mesh,
        in_specs=(
            P("scen", "tile", None),
            P("tile", None),
            P("tile", None),
            P(),
            P("scen"),
            P("tile"),
            P("tile"),
            P("tile"),
            P("tile", None),
            P("tile"),
            P("tile", None),
            P("tile"),
            P("tile", None),
            P("tile"),
        ),
        out_specs=(
            P("scen", "tile"),
            P("tile", None),
            P("tile"),
            P("tile", None),
            P("tile"),
            P("tile", None),
            P("tile"),
        ),
        check_vma=False,
    )
```

```python
import math

import jax
import jax.numpy as jnp
from jax import lax
from jax.experimental import pallas as pl
from jax.experimental.pallas import tpu as pltpu
from jax.sharding import PartitionSpec as P

BF = jnp.bfloat16
F32 = jnp.float32
HIGH = lax.Precision.HIGHEST
TILES = 64
SCENS = 4
STRIDES = {"zh": 16, "x": 4, "y": 1}


def dot(left, right, contract, precision=None):
    return lax.dot_general(
        left, right, (contract, ((), ())), precision=precision, preferred_element_type=F32
    )


def position(axis):
    return (lax.axis_index("tile") // STRIDES[axis]) % 4


def from_ahead(block, axis, ahead):
    stride = STRIDES[axis]
    pairs = []
    for target in range(TILES):
        mine = target // stride % 4
        pairs.append((target + ((mine + ahead) % 4 - mine) * stride, target))
    return lax.ppermute(block, "tile", pairs)


def pieces(block, axis):
    return [block] + [from_ahead(block, axis, ahead) for ahead in (1, 2, 3)]


def place(blocks, axis, dim):
    shape = list(blocks[0].shape)
    shape[dim] *= 4
    whole = jnp.zeros(shape, blocks[0].dtype)
    mine = position(axis)
    for ahead, block in enumerate(blocks):
        start = ((mine + ahead) % 4) * block.shape[dim]
        whole = lax.dynamic_update_slice_in_dim(whole, block, start, axis=dim)
    return whole


def exchange(parts):
    return lax.all_to_all(parts, "tile", 0, 0, tiled=True)


def to_all(block):
    return exchange(jnp.broadcast_to(block[None], (TILES,) + block.shape))


CHUNK = 16
ROW_SETS = (
    ((0, 4), (1, 5), (2, 6), (3, 7), (4, 8)),
    ((4, 8), (3, 9), (2, 10), (3, 9), (4, 8)),
    ((8, 12), (7, 11), (6, 10), (5, 9), (4, 8)),
)


def spread_kernel(diff_ref, recharge_ref, cells_ref, high_ref, low_ref, sum_ref, charge_ref):
    width = diff_ref.shape[1]
    column = lax.broadcasted_iota(jnp.int32, (CHUNK, width), 1)
    lane = lax.broadcasted_iota(jnp.int32, (CHUNK, 128), 1)
    for part in range(3):
        sets = ROW_SETS[part]

        def chunk(index, carry, part=part, sets=sets):
            at = pl.multiple_of(part * 64 + index * CHUNK, CHUNK)
            cells = cells_ref[pl.ds(at, CHUNK), :]
            own_row = cells >> 9
            hit = column == (cells & (width - 1))
            values = {
                row: jnp.where(hit & (own_row == row - 4 * part), 1.0, 0.0)
                for row in range(*sets[0])
            }
            sums = {}
            charge = jnp.zeros((CHUNK, 128), F32)
            for step in range(5):
                if step < 4:
                    product = None
                    for row in range(4, 8):
                        if row in values:
                            v = values[row]
                            sums[row] = sums[row] + v if row in sums else v
                            term = v * recharge_ref[row - 4 : row - 3, :]
                            product = term if product is None else product + term
                    if product is not None:
                        total = jnp.sum(product, axis=1, keepdims=True)
                        charge = jnp.where(lane == step, total, charge)
                    weighted = {row: v * diff_ref[row : row + 1, :] for row, v in values.items()}
                    later = {}
                    for row in range(*sets[step + 1]):
                        out = values.get(row)
                        if row in weighted:
                            w = weighted[row]
                            left = jnp.where(column == 0, 0.0, pltpu.roll(w, 1, 1))
                            right = jnp.where(column == width - 1, 0.0, pltpu.roll(w, width - 1, 1))
                            out = out + (left + right - 4.0 * w)
                        for near in (row - 1, row + 1):
                            if near in weighted:
                                out = weighted[near] if out is None else out + weighted[near]
                        later[row] = out
                    values = later
            for row in range(4, 8):
                columns = slice((row - 4) * width, (row - 3) * width)
                v = values[row]
                high = v.astype(BF)
                high_ref[pl.ds(at, CHUNK), columns] = high
                low_ref[pl.ds(at, CHUNK), columns] = (v - high.astype(F32)).astype(BF)
                sum_ref[pl.ds(at, CHUNK), columns] = sums.get(row, jnp.zeros_like(v))
            charge_ref[pl.ds(at, CHUNK), :] = charge
            return carry

        lax.fori_loop(0, 64 // CHUNK, chunk, 0)


def spread_operator(diffusivity, recharge_map, cells):
    monitors = cells.shape[0]
    flat = recharge_map.shape[0] * recharge_map.shape[1]
    return pl.pallas_call(
        spread_kernel,
        out_shape=(
            jax.ShapeDtypeStruct((monitors, flat), BF),
            jax.ShapeDtypeStruct((monitors, flat), BF),
            jax.ShapeDtypeStruct((monitors, flat), F32),
            jax.ShapeDtypeStruct((monitors, 128), F32),
        ),
        compiler_params=pltpu.CompilerParams(vmem_limit_bytes=24 * 1024 * 1024),
        cost_estimate=pl.CostEstimate(
            flops=30_000_000, bytes_accessed=4_000_000, transcendentals=0
        ),
    )(diffusivity, recharge_map, cells)


def per_device(
    initial_heads,
    diffusivity,
    recharge_map,
    rate_table,
    recharge_ids,
    monitor_cells,
    well_cells,
    targets,
    w_in,
    b_in,
    w_mid,
    b_mid,
    w_out,
    b_out,
):
    members, rows, cols = initial_heads.shape
    cells = rows * cols
    scen = lax.axis_index("scen")
    tile = lax.axis_index("tile")
    positions = jnp.arange(cells, dtype=jnp.int32)
    heads = initial_heads.reshape(members, cells)

    with jax.named_scope("first_layer"):
        monitor_pick = (monitor_cells[:, None] == positions[None, :]).astype(BF)
        observed = dot(heads, monitor_pick, ((1,), (1,))).astype(BF)
        first_terms = dot(observed, w_in, ((1,), (0,))).astype(BF)
        first_terms = exchange(first_terms.reshape(TILES, 32, 128))

    with jax.named_scope("biases"):
        small = jnp.zeros((8, 128), F32)
        small = small.at[0, :72].set(jnp.concatenate([b_in, b_mid, b_out]))
        small = small.at[1, :64].set(targets)
        small = to_all(small)
        b_in_all = small[:, 0, :32].reshape(2048)
        b_mid_all = small[:, 0, 32:64].reshape(2048)
        b_out_all = small[:, 0, 64:72].reshape(512)
        targets_all = small[:, 1, :64]

    with jax.named_scope("weights"):
        mid = lax.dynamic_slice_in_dim(w_mid, scen * 512, 512, axis=1)
        mid = place(pieces(mid[None], "zh"), "zh", 0)
        mid = place(pieces(mid[:, None], "y"), "y", 1).reshape(512, 512)
        mids = pieces(mid, "x")
        swap = []
        for s in range(SCENS):
            for z in range(4):
                for r in range(16):
                    swap.append((z * TILES + s * 16 + r, s * TILES + z * 16 + r))
        last = lax.ppermute(w_out, ("scen", "tile"), swap)
        last = place(pieces(last, "y"), "y", 0)
        last = place(pieces(last, "x"), "x", 0)

    with jax.named_scope("operator"):
        slab = jnp.concatenate(
            [diffusivity, jnp.pad((monitor_cells + 1).astype(F32), (0, cols - 64))[None]], axis=0
        )
        down = [(i, i + 1) for i in range(TILES - 1)]
        before = lax.ppermute(slab, "tile", down)
        after = lax.ppermute(slab, "tile", [(b, a) for a, b in down])
        near_cells = jnp.concatenate([before[4, :64], slab[4, :64], after[4, :64]])
        near_cells = near_cells.astype(jnp.int32) - 1
        near_diff = jnp.concatenate([before[:4], diffusivity, after[:4]], axis=0)
        high, low, summed, charge = spread_operator(near_diff, recharge_map, near_cells[:, None])
        well_hot = (well_cells[:, None] == positions[None, :]).astype(F32)
        coupling = dot(well_hot, summed, ((1,), (1,)), HIGH)
        codes = jnp.arange(rate_table.shape[0], dtype=jnp.int32)
        pattern_hot = (recharge_ids[:, None] == codes[None, :]).astype(F32)
        monthly = dot(pattern_hot, rate_table, ((1,), (0,)), HIGH)
        backward_charge = jnp.stack([charge[:, 3], charge[:, 2], charge[:, 1], charge[:, 0]])
        still = (
            dot(heads, high, ((1,), (1,)))
            + dot(heads, low, ((1,), (1,)))
            + dot(monthly, backward_charge, ((1,), (0,)), HIGH)
        )
        still = still.reshape(TILES, 2, 3, 64).transpose(0, 2, 1, 3).reshape(TILES, 3, 128)
        coupling = coupling.reshape(8, 3, 64).transpose(1, 0, 2).reshape(12, 128)
        sent = jnp.concatenate(
            [
                still,
                jnp.broadcast_to(coupling[None], (TILES, 12, 128)),
                jnp.zeros((TILES, 1, 128), F32),
            ],
            axis=1,
        )
        got = exchange(sent)
        none = jnp.zeros((1, 128), F32)
        still = (
            got[:, 1]
            + jnp.concatenate([none, got[:-1, 2]], axis=0)
            + jnp.concatenate([got[1:, 0], none], axis=0)
        )
        coupling = got[:, 3:15].reshape(TILES, 3, 8, 64).transpose(0, 2, 1, 3).reshape(512, 192)

    with jax.named_scope("act1"):
        first_pre = jnp.sum(first_terms.astype(F32), axis=0)
        act1 = jnp.tanh(first_pre.reshape(2, 2048) + b_in_all[None, :]).astype(BF)
        shared = jnp.concatenate([act1.reshape(32, 128), observed.reshape(TILES, 128)], axis=0)
        shared = lax.all_gather(shared, "scen", axis=0, tiled=False)
        act1 = shared[:, :32].reshape(8, 2048)
        observed_all = shared[:, 32:].reshape(SCENS, TILES, 2, 64).transpose(1, 0, 2, 3)
        observed_all = observed_all.reshape(512, 64)

    with jax.named_scope("act2"):
        here = position("x")
        act1_x = act1.reshape(8, 4, 4, 128)
        middle_pre = lax.dynamic_slice_in_dim(b_mid_all, scen * 512, 512)[None, :]
        for ahead in range(4):
            part = lax.dynamic_slice_in_dim(act1_x, (here + ahead) % 4, 1, axis=2)
            middle_pre = middle_pre + dot(part.reshape(8, 512), mids[ahead], ((1,), (0,)))
        act2 = jnp.tanh(middle_pre).astype(BF)

    with jax.named_scope("pre3"):
        terms = dot(act2, last, ((1,), (0,)))
        shared = jnp.concatenate(
            [terms.reshape(32, 128), act2.astype(F32).reshape(32, 128), still], axis=0
        )
        shared = lax.all_gather(shared, "scen", axis=0, tiled=False)
        pre3 = jnp.sum(shared[:, :32], axis=0).reshape(8, 512) + b_out_all[None, :]
        act2_all = shared[:, 32:64].reshape(SCENS, 8, 512).astype(BF)
        still = shared[:, 64:].reshape(SCENS, TILES, 2, 64).transpose(1, 0, 2, 3)
        still = still.reshape(TILES, 8, 64)

    with jax.named_scope("wells"):
        rates = 0.5 * jax.nn.softplus(pre3)
        owner = lax.broadcasted_iota(jnp.int32, (TILES, 1, 512), 2) // 8
        at_tile = owner == lax.broadcasted_iota(jnp.int32, (TILES, 1, 512), 0)
        by_tile = jnp.where(at_tile, rates[None], 0.0).reshape(512, 512)
        drawn = dot(by_tile, coupling, ((1,), (0,)), HIGH).reshape(TILES, 8, 192)
        blank = jnp.zeros((1, 8, 64), F32)
        sink = (
            drawn[:, :, 64:128]
            + jnp.concatenate([blank, drawn[:-1, :, 128:]], axis=0)
            + jnp.concatenate([drawn[1:, :, :64], blank], axis=0)
        )
        final = (still - sink).astype(BF)
        spread = (final.astype(F32) - targets_all[:, None, :]) / math.sqrt(512)
        wide = jnp.concatenate(
            [
                jnp.concatenate([blank, spread[:-1]], axis=0),
                spread,
                jnp.concatenate([spread[1:], blank], axis=0),
            ],
            axis=2,
        ).reshape(512, 192)
        total = dot(wide, coupling, ((1,), (1,)), HIGH).reshape(TILES, 8, 512)
        total = jnp.sum(jnp.where(at_tile, total, 0.0), axis=0)
        g3 = (-total * 0.5 * jax.nn.sigmoid(pre3)).astype(BF)

    with jax.named_scope("g2"):
        act2_f = act2.astype(F32)
        g2 = (dot(g3, last, ((1,), (1,))) * (1.0 - act2_f * act2_f)).astype(BF)

    with jax.named_scope("regroup"):
        act2_full = act2_all.transpose(1, 0, 2).reshape(8, 2048)
        by_row = jnp.stack([act1, act2_full]).reshape(2, 8, TILES, 32)
        by_row = by_row.transpose(2, 0, 1, 3).reshape(TILES, 4, 128)
        my_final = lax.dynamic_slice_in_dim(final, scen * 2, 2, axis=1).reshape(TILES, 1, 128)
        my_g3 = lax.dynamic_slice_in_dim(g3, scen * 128, 128, axis=1)
        grads = jnp.concatenate([g2.reshape(32, 128), my_g3], axis=0)
        sent = jnp.concatenate(
            [
                jnp.broadcast_to(grads[None], (TILES, 40, 128)),
                by_row,
                my_final,
                jnp.zeros((TILES, 3, 128), BF),
            ],
            axis=1,
        )
        got = exchange(sent)
        final_heads = got[:, 44].reshape(members, 64)

    with jax.named_scope("g1"):
        g1_terms = jnp.zeros((8, 4, 4, 128), F32)
        for ahead in range(4):
            part = dot(g2, mids[ahead], ((1,), (1,))).reshape(8, 4, 1, 128)
            g1_terms = lax.dynamic_update_slice_in_dim(
                g1_terms, part, (here + ahead) % 4, axis=2
            )
        g1_terms = g1_terms.reshape(8, 4, 512).transpose(1, 0, 2)
        g1_terms = lax.all_to_all(g1_terms, "scen", 0, 0, tiled=True)
        act1_f = lax.dynamic_slice_in_dim(act1, scen * 512, 512, axis=1).astype(F32)
        g1 = (jnp.sum(g1_terms, axis=0) * (1.0 - act1_f * act1_f)).astype(BF)
        g1_all = to_all(g1.reshape(32, 128)).reshape(512, 512)

    with jax.named_scope("weight_grads"):
        ones = jnp.ones((512, 8), BF)
        g2_all = got[:, :32].reshape(512, 512)
        g3_all = got[:, 32:40].reshape(512, 128)
        act1_own = jnp.concatenate([got[:, 40:42].reshape(512, 32), ones], axis=1)
        act2_own = jnp.concatenate([got[:, 42:44].reshape(512, 32), ones], axis=1)
        both = jnp.concatenate(
            [dot(act1_own, g2_all, ((0,), (0,))), dot(act2_own, g3_all, ((0,), (0,)))], axis=1
        )
        both = lax.all_gather(both, "scen", axis=0, tiled=False)
        g_w_mid = both[:, :, :512].transpose(1, 0, 2).reshape(40, 2048)
        g_w_out = both[:, :, 512:].transpose(1, 0, 2).reshape(40, 512)
        observed_own = jnp.concatenate([observed_all, ones], axis=1)
        g_w_in = dot(observed_own, g1_all, ((0,), (0,)))
        g_w_in = lax.all_gather(g_w_in, "scen", axis=1, tiled=True)
        g_b_in = lax.dynamic_slice_in_dim(g_w_in[64], tile * 32, 32)
        g_b_mid = lax.dynamic_slice_in_dim(g_w_mid[32], tile * 32, 32)
        g_b_out = lax.dynamic_slice_in_dim(g_w_out[32], tile * 8, 8)
    return (final_heads, g_w_in[:64], g_b_in, g_w_mid[:32], g_b_mid, g_w_out[:32], g_b_out)


def solution(mesh):
    return jax.shard_map(
        per_device,
        mesh=mesh,
        in_specs=(
            P("scen", "tile", None),
            P("tile", None),
            P("tile", None),
            P(),
            P("scen"),
            P("tile"),
            P("tile"),
            P("tile"),
            P("tile", None),
            P("tile"),
            P("tile", None),
            P("tile"),
            P("tile", None),
            P("tile"),
        ),
        out_specs=(
            P("scen", "tile"),
            P("tile", None),
            P("tile"),
            P("tile", None),
            P("tile"),
            P("tile", None),
            P("tile"),
        ),
        check_vma=False,
    )
```
